1024 devices in a mesh: shard: 64 (over z_hi, y, x), replica: 16 (over z_lo, core).
Axes of the slice: x: 4, y: 4, z: 32 (z_hi: 4, z_lo: 8; z = z_hi * 8 + z_lo), core: 2. Of those that a mesh axis runs over, the one named last changes fastest.
Arguments:
- gradient: bfloat16 [16, 5120, 13824], P('replica', None, 'shard'), as said below
- projection: float32 [5120, 128], replicated, as said below
- first_moment: float32 [128, 13824], P(None, 'shard'), may hold values from -8 to 8
- second_moment: float32 [128, 13824], P(None, 'shard'), as said below
- weight: float32 [5120, 13824], P('replica', 'shard'), as said below
Outputs:
- update: float32 [5120, 13824], P('replica', 'shard')
- new_first: float32 [128, 13824], P(None, 'shard')
- new_second: float32 [128, 13824], P(None, 'shard')
The draws below stay inside these ranges and needn't reach their ends.
Inputs may be any that keep to these rules, and one draw needn't show every extreme that they name: Real-valued gradient partials of order one. `projection`: Real-valued entries of order one over the square root of 5120. `second_moment`: positive entries. `weight`: Real-valued entries of order one.
All inputs are finite; a program needn't handle non-finite values.
Results may differ from the reference program's by a relative error of at most 0.0015.
The reference program's roundings to bfloat16 on the way (of `low_projection`) count: a program that leaves them out, or rounds other values in their place, can miss the bound.
Values sent between devices are 32-bit elements; how exact they have to be, the bound alone decides.
No kernel may reach another device: no remote copies, remote signals or barrier semaphores. Data moves between devices by JAX's collectives and lax.ppermute only.
A program may use at most 32 MiB of HBM per device.

```python
import math
import jax
import jax.numpy as jnp
from jax import lax

D = 5120
FFW = 13824
RANK = 128
ADAM_STEP = 10
N_REPLICA = 16


def spread_scales(key, shape, decades):
    return jnp.exp(jax.random.uniform(key, shape, jnp.float32) * (decades * math.log(10.0)))


def draw_gradient(key, part):
    key = jax.random.fold_in(key, 11)
    key_rows, key_cols, key_noise = jax.random.split(key, 3)
    row_scale = spread_scales(key_rows, (1, D, 1), 1.0)
    col_ramp = jnp.exp(math.log(3.0) * jnp.arange(FFW, dtype=jnp.float32) / FFW)
    col_scale = spread_scales(key_cols, (1, 1, FFW), 1.0) * col_ramp[None, None, :]
    rep_scale = jnp.exp(math.log(3.0) * jnp.arange(N_REPLICA, dtype=jnp.float32) / max(N_REPLICA - 1, 1))[:, None, None]
    noise = jnp.clip(jax.random.normal(key_noise, (N_REPLICA, D, FFW), jnp.float32), -6.0, 6.0)
    values = noise * row_scale * col_scale * rep_scale / (4.6 * math.sqrt(N_REPLICA))
    return values.astype(jnp.bfloat16)


def draw_projection(key, part):
    key = jax.random.fold_in(key, 23)
    key_rows, key_noise = jax.random.split(key, 2)
    row_ramp = jnp.exp(math.log(3.0) * jnp.arange(D, dtype=jnp.float32) / D)
    row_scale = spread_scales(key_rows, (D, 1), 1.0) * row_ramp[:, None]
    noise = jnp.clip(jax.random.normal(key_noise, (D, RANK), jnp.float32), -6.0, 6.0)
    return noise * row_scale / (4.6 * math.sqrt(D))


def draw_second_moment(key, part):
    key = jax.random.fold_in(key, 37)
    key_cols = jax.random.fold_in(key, 0)
    key_noise = jax.random.fold_in(key, 2)
    col_ramp = jnp.exp(-2.0 * math.log(3.0) * jnp.arange(FFW, dtype=jnp.float32) / FFW)
    col_scale = spread_scales(key_cols, (1, FFW), 2.0) * col_ramp[None, :]
    noise = jax.random.uniform(key_noise, (RANK, FFW), jnp.float32, 0.5, 1.5)
    return noise * col_scale


def draw_weight(key, part):
    key = jax.random.fold_in(key, 41)
    key_rows, key_cols, key_noise = jax.random.split(key, 3)
    row_ramp = jnp.exp(math.log(3.0) * jnp.arange(D, dtype=jnp.float32) / D)
    col_ramp = jnp.exp(math.log(3.0) * jnp.arange(FFW, dtype=jnp.float32) / FFW)
    row_scale = spread_scales(key_rows, (D, 1), 1.0) * row_ramp[:, None]
    col_scale = spread_scales(key_cols, (1, FFW), 1.0) * col_ramp[None, :]
    noise = jnp.clip(jax.random.normal(key_noise, (D, FFW), jnp.float32), -6.0, 6.0)
    return noise * row_scale * col_scale / 21.0


def level_of(own_key, extent, shards, least, largest):
    level, own = 1.0, jax.random.fold_in(own_key, 6)
    for position, blocks in shards:
        heights = jnp.exp(jax.random.uniform(jax.random.fold_in(own, position), (blocks,), jnp.float32, least / len(shards), largest / len(shards)))
        level = level * jnp.repeat(heights, extent[position] // blocks).reshape([-1 if axis == position else 1 for axis in range(len(extent))])
    return level


def gaussian(key, shape, deviation, most, cuts=(), kind=jnp.bfloat16):
    entries = deviation * jax.random.normal(key, shape, jnp.float32)
    if cuts:
        entries = entries * level_of(key, shape, cuts, -0.22, 0.18)
    return jnp.clip(entries, -most, most).astype(kind)


def setup_inputs(seed: int = 0) -> dict:
    splits = jax.random.split(jax.random.key(seed), 6)
    gradient = draw_gradient(jax.random.fold_in(splits[5], 71), 0)
    projection = draw_projection(jax.random.fold_in(splits[5], 71), 0)
    first_moment = gaussian(splits[2], (RANK, FFW), 2.0, 8.0, ((1, 64),), jnp.float32)
    second_moment = draw_second_moment(jax.random.fold_in(splits[5], 71), 0)
    weight = draw_weight(jax.random.fold_in(splits[5], 71), 0)
    return {"gradient": gradient, "projection": projection, "first_moment": first_moment, "second_moment": second_moment, "weight": weight}


def reference(gradient, projection, first_moment, second_moment, weight):
    low_projection = projection.astype(jnp.bfloat16)

    def add_partial(total, partial_value):
        term = lax.dot_general(low_projection, partial_value, (((0,), (0,)), ((), ())), preferred_element_type=jnp.float32)
        return (total + term, None)
    start_total = jnp.zeros((projection.shape[1], gradient.shape[2]), jnp.float32)
    low_grad, unused = lax.scan(add_partial, start_total, gradient)
    new_first = 0.9 * first_moment + 0.1 * low_grad
    new_second = 0.95 * second_moment + 0.05 * low_grad * low_grad
    first_fix = 1.0 - 0.9 ** ADAM_STEP
    second_fix = 1.0 - 0.95 ** ADAM_STEP
    normalized = new_first / first_fix / (jnp.sqrt(new_second / second_fix) + 1e-08)
    full_step = jnp.dot(projection, normalized, precision=lax.Precision.HIGHEST, preferred_element_type=jnp.float32)
    weight_sq = jnp.sum(weight * weight)
    step_sq = jnp.sum(full_step * full_step)
    update = full_step * (jnp.sqrt(weight_sq) / (jnp.sqrt(step_sq) + 1e-06))
    return (update, new_first, new_second)
```

```python
import jax
import jax.numpy as jnp
from jax import lax
from jax.sharding import Mesh, PartitionSpec as P

ADAM_STEP = 10
SHARD = ("h1", "h0", "y1", "y0", "x1", "x0")
REPLICA = ("l2", "l1", "l0", "c")


def adam_update(low_grad, first_moment, second_moment):
    new_first = 0.9 * first_moment + 0.1 * low_grad
    new_second = 0.95 * second_moment + 0.05 * low_grad * low_grad
    first_fix = 1.0 - 0.9**ADAM_STEP
    second_fix = 1.0 - 0.95**ADAM_STEP
    normalized = new_first / first_fix / (jnp.sqrt(new_second / second_fix) + 1e-08)
    return (new_first, new_second, normalized)


def pair_sum(x, axis):
    both = lax.all_gather(x, axis, axis=0, tiled=False)
    return both[0] + both[1]


def shards(gradient, projection, first_moment, second_moment, weight):
    rows_here, columns = weight.shape
    rank = projection.shape[1]
    low_projection = projection.astype(jnp.bfloat16)
    partial = lax.dot_general(
        low_projection, gradient[0], (((0,), (0,)), ((), ())), preferred_element_type=jnp.float32
    )
    weight_part = jnp.sum(weight * weight)
    total = jnp.concatenate([partial, jnp.broadcast_to(weight_part, (rank, 256 - columns))], axis=1)
    for axis in ("c", "l0", "l1", "l2"):
        total = pair_sum(total, axis)
    low_grad = total[:, :columns]
    new_first, new_second, normalized = adam_update(low_grad, first_moment, second_moment)

    position = lax.axis_index(REPLICA)
    own_projection = lax.dynamic_slice_in_dim(projection, position * rows_here, rows_here, 0)
    step = jnp.dot(
        own_projection, normalized, precision=lax.Precision.HIGHEST, preferred_element_type=jnp.float32
    )
    shard_step = jnp.dot(
        projection, normalized, precision=lax.Precision.HIGH, preferred_element_type=jnp.float32
    )
    step_part = jnp.sum(shard_step * shard_step)
    lane = lax.broadcasted_iota(jnp.int32, (1, 128), 1)
    message = jnp.where(lane == 0, step_part, total[:1, 128:])
    shards_total = lax.axis_size(SHARD)
    parts = lax.all_to_all(
        jnp.broadcast_to(message[None], (shards_total, 1, 128)), SHARD, 0, 0
    )
    sums = jnp.sum(parts, axis=(0, 1))
    scale = jnp.sqrt(sums[127]) / (jnp.sqrt(sums[0]) + 1e-06)
    return (step * scale, new_first, new_second)


def solution(mesh):
    fine = Mesh(mesh.devices.reshape((2,) * 10), SHARD + REPLICA)
    placed = (
        P(REPLICA, None, SHARD),
        P(),
        P(None, SHARD),
        P(None, SHARD),
        P(REPLICA, SHARD),
    )
    return jax.shard_map(
        shards,
        mesh=fine,
        in_specs=placed,
        out_specs=(P(REPLICA, SHARD), P(None, SHARD), P(None, SHARD)),
        check_vma=False,
    )
```

```python
import functools

import jax
import jax.numpy as jnp
from jax import lax
from jax.experimental import pallas as pl
from jax.experimental.pallas import tpu as pltpu
from jax.sharding import Mesh, PartitionSpec as P

ADAM_STEP = 10
PLANE = ("y1", "y0", "x1", "x0")
BLOCKS = ("h1", "h0")
SHARD = BLOCKS + PLANE
REPLICA = ("l2", "l1", "l0", "c")
SUBLANES, LANES = 8, 128
MIB = 2**20


def partial_kernel(chunks, gradient, projection, weight, out, grad_v, proj_v, weight_v, sems):
    columns, depth = grad_v.shape
    depth //= chunks
    copies = []
    for i in range(chunks):
        part = pl.ds(i * depth, depth)
        copies.append(
            (
                pltpu.make_async_copy(projection.at[part], proj_v.at[part], sems.at[0, i]),
                pltpu.make_async_copy(gradient.at[:, part], grad_v.at[:, part], sems.at[1, i]),
            )
        )
        for copy in copies[-1]:
            copy.start()
    weight_copy = pltpu.make_async_copy(weight, weight_v, sems.at[2, 0])
    weight_copy.start()
    total = None
    for i in range(chunks):
        for copy in copies[i]:
            copy.wait()
        part = slice(i * depth, (i + 1) * depth)
        term = jnp.dot(
            grad_v[:, part], proj_v[part].astype(jnp.bfloat16), preferred_element_type=jnp.float32
        )
        total = term if total is None else total + term
    out[:columns] = total
    weight_copy.wait()
    weight_sq = jnp.sum(weight_v[...] * weight_v[...])
    out[columns:] = jnp.full((out.shape[0] - columns, out.shape[1]), weight_sq, jnp.float32)


def partial_grad(gradient, projection, weight):
    columns, depth = gradient.shape
    rank = projection.shape[1]
    chunks = 8
    anywhere = pl.BlockSpec(memory_space=pl.ANY)
    return pl.pallas_call(
        functools.partial(partial_kernel, chunks),
        out_shape=jax.ShapeDtypeStruct((columns + SUBLANES, rank), jnp.float32),
        in_specs=[anywhere] * 3,
        out_specs=pl.BlockSpec(memory_space=pltpu.VMEM),
        scratch_shapes=[
            pltpu.VMEM(gradient.shape, gradient.dtype),
            pltpu.VMEM(projection.shape, projection.dtype),
            pltpu.VMEM(weight.shape, weight.dtype),
            pltpu.SemaphoreType.DMA((3, chunks)),
        ],
        compiler_params=pltpu.CompilerParams(vmem_limit_bytes=48 * MIB),
    )(gradient, projection, weight)


def split(x):
    high = x.astype(jnp.bfloat16)
    low = (x - high.astype(jnp.float32)).astype(jnp.bfloat16)
    return high, low


def dot_rows(left, right):
    return lax.dot_general(
        left, right, (((1,), (1,)), ((), ())), preferred_element_type=jnp.float32
    )


def adam_kernel(total, first, second, projection, new_first, new_second, normal, message):
    columns = first.shape[0]
    low_grad = total[:columns]
    moment = 0.9 * first[...] + 0.1 * low_grad
    square = 0.95 * second[...] + 0.05 * low_grad * low_grad
    new_first[...] = moment
    new_second[...] = square
    first_fix = 1.0 - 0.9**ADAM_STEP
    second_fix = 1.0 - 0.95**ADAM_STEP
    normalized = moment / first_fix / (jnp.sqrt(square / second_fix) + 1e-08)
    normal[...] = normalized
    high, low = split(normalized)
    twice = jnp.concatenate([high, high], axis=1)
    depth = 512
    squares = jnp.zeros((SUBLANES, columns), jnp.float32)
    for i in range(projection.shape[0] // depth):
        left, left_low = split(projection[i * depth : (i + 1) * depth])
        step = dot_rows(jnp.concatenate([left, left_low], axis=1), twice) + dot_rows(left, low)
        squares += jnp.sum((step * step).reshape(depth // SUBLANES, SUBLANES, columns), axis=0)
    step_sq = jnp.sum(squares)
    lane = lax.broadcasted_iota(jnp.int32, (1, LANES), 1)
    row = jnp.where(lane == 0, step_sq, total[columns : columns + 1])
    message[...] = jnp.broadcast_to(row[None], message.shape)


def adam_and_norm(total, first, second, projection, partners):
    vmem = pl.BlockSpec(memory_space=pltpu.VMEM)
    shape = jax.ShapeDtypeStruct(first.shape, jnp.float32)
    return pl.pallas_call(
        adam_kernel,
        out_shape=(shape, shape, shape, jax.ShapeDtypeStruct((partners, 1, LANES), jnp.float32)),
        in_specs=[vmem] * 4,
        out_specs=(vmem,) * 4,
        compiler_params=pltpu.CompilerParams(vmem_limit_bytes=24 * MIB),
    )(total, first, second, projection)


def scale_kernel(sums, step, update):
    weight_sq = jnp.broadcast_to(sums[:, 1:2], (1, step.shape[1]))
    step_sq = jnp.broadcast_to(sums[:, :1], (1, step.shape[1]))
    update[...] = step[...] * (jnp.sqrt(weight_sq) / (jnp.sqrt(step_sq) + 1e-06))


def scaled(sums, step):
    vmem = pl.BlockSpec(memory_space=pltpu.VMEM)
    return pl.pallas_call(
        scale_kernel,
        out_shape=jax.ShapeDtypeStruct(step.shape, jnp.float32),
        in_specs=[vmem] * 2,
        out_specs=vmem,
        compiler_params=pltpu.CompilerParams(vmem_limit_bytes=16 * MIB),
    )(sums, step)


def pair_sum(x, axis):
    both = lax.all_gather(x, axis, axis=0, tiled=False)
    return both[0] + both[1]


def shards(gradient, projection, first_moment, second_moment, weight):
    rows_here = weight.shape[0]
    total = pair_sum(partial_grad(jnp.swapaxes(gradient, 1, 2)[0], projection, weight), "c")
    half = total.shape[0] // 2
    total = lax.dynamic_slice_in_dim(total, lax.axis_index("c") * half, half, 0)
    for axis in ("l0", "l1", "l2"):
        total = pair_sum(total, axis)
    total = lax.all_gather(total, "c", axis=0, tiled=True)

    new_first, new_second, normalized, message = adam_and_norm(
        total, first_moment.T, second_moment.T, projection, lax.axis_size(PLANE)
    )
    position = lax.axis_index(REPLICA)
    own_projection = lax.dynamic_slice_in_dim(projection, position * rows_here, rows_here, 0)
    step = jnp.dot(
        own_projection, normalized.T, precision=lax.Precision.HIGHEST, preferred_element_type=jnp.float32
    )
    parts = jnp.sum(lax.all_to_all(message, PLANE, 0, 0), axis=0)
    step, parts = lax.optimization_barrier((step, parts))
    sums = lax.psum(parts, BLOCKS)
    return (scaled(sums, step), new_first.T, new_second.T)


def solution(mesh):
    fine = Mesh(mesh.devices.reshape((2,) * 10), SHARD + REPLICA)
    placed = (
        P(REPLICA, None, SHARD),
        P(),
        P(None, SHARD),
        P(None, SHARD),
        P(REPLICA, SHARD),
    )
    return jax.shard_map(
        shards,
        mesh=fine,
        in_specs=placed,
        out_specs=(P(REPLICA, SHARD), P(None, SHARD), P(None, SHARD)),
        check_vma=False,
    )
```

```python
import functools

import jax
import jax.numpy as jnp
from jax import lax
from jax.experimental import pallas as pl
from jax.experimental.pallas import tpu as pltpu
from jax.sharding import Mesh, PartitionSpec as P

ADAM_STEP = 10
PLANE = ("y1", "y0", "x1", "x0")
BLOCKS = ("h1", "h0")
SHARD = BLOCKS + PLANE
REPLICA = ("l2", "l1", "l0", "c")
SUBLANES, LANES = 8, 128
MIB = 2**20


def partial_kernel(chunks, gradient, projection, weight, out, grad_v, proj_v, weight_v, sems):
    columns, depth = grad_v.shape
    depth //= chunks
    copies = []
    for i in range(chunks):
        part = pl.ds(i * depth, depth)
        copies.append(
            (
                pltpu.make_async_copy(projection.at[part], proj_v.at[part], sems.at[0, i]),
                pltpu.make_async_copy(gradient.at[:, part], grad_v.at[:, part], sems.at[1, i]),
            )
        )
        for copy in copies[-1]:
            copy.start()
    weight_copy = pltpu.make_async_copy(weight, weight_v, sems.at[2, 0])
    weight_copy.start()
    total = None
    for i in range(chunks):
        for copy in copies[i]:
            copy.wait()
        part = slice(i * depth, (i + 1) * depth)
        term = jnp.dot(
            grad_v[:, part], proj_v[part].astype(jnp.bfloat16), preferred_element_type=jnp.float32
        )
        total = term if total is None else total + term
    out[:columns] = total
    weight_copy.wait()
    weight_sq = jnp.sum(weight_v[...] * weight_v[...])
    out[columns:] = jnp.full((out.shape[0] - columns, out.shape[1]), weight_sq, jnp.float32)


def partial_grad(gradient, projection, weight):
    columns, depth = gradient.shape
    rank = projection.shape[1]
    chunks = 5
    anywhere = pl.BlockSpec(memory_space=pl.ANY)
    return pl.pallas_call(
        functools.partial(partial_kernel, chunks),
        out_shape=jax.ShapeDtypeStruct((columns + SUBLANES, rank), jnp.float32),
        in_specs=[anywhere] * 3,
        out_specs=pl.BlockSpec(memory_space=pltpu.VMEM),
        scratch_shapes=[
            pltpu.VMEM(gradient.shape, gradient.dtype),
            pltpu.VMEM(projection.shape, projection.dtype),
            pltpu.VMEM(weight.shape, weight.dtype),
            pltpu.SemaphoreType.DMA((3, chunks)),
        ],
        compiler_params=pltpu.CompilerParams(vmem_limit_bytes=60 * MIB),
    )(gradient, projection, weight)


def split(x):
    high = x.astype(jnp.bfloat16)
    low = (x - high.astype(jnp.float32)).astype(jnp.bfloat16)
    return high, low


def dot_rows(left, right):
    return lax.dot_general(
        left, right, (((1,), (1,)), ((), ())), preferred_element_type=jnp.float32
    )


def adam_kernel(total, first, second, projection, new_first, new_second, normal, message):
    columns = first.shape[0]
    low_grad = total[:columns]
    moment = 0.9 * first[...] + 0.1 * low_grad
    square = 0.95 * second[...] + 0.05 * low_grad * low_grad
    new_first[...] = moment
    new_second[...] = square
    first_fix = 1.0 - 0.9**ADAM_STEP
    second_fix = 1.0 - 0.95**ADAM_STEP
    normalized = moment / first_fix / (jnp.sqrt(square / second_fix) + 1e-08)
    normal[...] = normalized
    high, low = split(normalized)
    twice = jnp.concatenate([high, high], axis=1)
    depth = 512
    squares = jnp.zeros((SUBLANES, columns), jnp.float32)
    for i in range(projection.shape[0] // depth):
        left, left_low = split(projection[i * depth : (i + 1) * depth])
        step = dot_rows(jnp.concatenate([left, left_low], axis=1), twice) + dot_rows(left, low)
        squares += jnp.sum((step * step).reshape(depth // SUBLANES, SUBLANES, columns), axis=0)
    step_sq = jnp.sum(squares)
    lane = lax.broadcasted_iota(jnp.int32, (1, LANES), 1)
    row = jnp.where(lane == 0, step_sq, total[columns : columns + 1])
    message[...] = jnp.broadcast_to(row[None], message.shape)


def adam_and_norm(total, first, second, projection, partners):
    vmem = pl.BlockSpec(memory_space=pltpu.VMEM)
    shape = jax.ShapeDtypeStruct(first.shape, jnp.float32)
    return pl.pallas_call(
        adam_kernel,
        out_shape=(shape, shape, shape, jax.ShapeDtypeStruct((partners, 1, LANES), jnp.float32)),
        in_specs=[vmem] * 4,
        out_specs=(vmem,) * 4,
        compiler_params=pltpu.CompilerParams(vmem_limit_bytes=24 * MIB),
    )(total, first, second, projection)


def scale_kernel(sums, step, update):
    weight_sq = jnp.broadcast_to(sums[:, 1:2], (1, step.shape[1]))
    step_sq = jnp.broadcast_to(sums[:, :1], (1, step.shape[1]))
    update[...] = step[...] * (jnp.sqrt(weight_sq) / (jnp.sqrt(step_sq) + 1e-06))


def scaled(sums, step):
    vmem = pl.BlockSpec(memory_space=pltpu.VMEM)
    return pl.pallas_call(
        scale_kernel,
        out_shape=jax.ShapeDtypeStruct(step.shape, jnp.float32),
        in_specs=[vmem] * 2,
        out_specs=vmem,
        compiler_params=pltpu.CompilerParams(vmem_limit_bytes=16 * MIB),
    )(sums, step)


def pair_sum(x, axis):
    both = lax.all_gather(x, axis, axis=0, tiled=False)
    return both[0] + both[1]


def block_permute(x, source, target, mirrored=False):
    ring = BLOCKS + REPLICA
    chips, cores = lax.axis_size(REPLICA[:3]), lax.axis_size("c")
    pairs = []
    for chip in range(chips):
        other = chips - 1 - chip if mirrored else chip
        for core in range(cores):
            pairs.append(
                ((source * chips + chip) * cores + core, (target * chips + other) * cores + core)
            )
    return lax.ppermute(x, ring, pairs)


def blocks_sum(x):
    total = x
    for term in (block_permute(x, 2, 0, True), block_permute(x, 1, 0), block_permute(x, 3, 0)):
        total = total + term
    spread = [block_permute(total, 0, target) for target in (2, 1, 3)]
    return jnp.where(lax.axis_index(BLOCKS) == 0, total, spread[0] + spread[1] + spread[2])


def shards(gradient, projection, first_moment, second_moment, weight):
    rows_here = weight.shape[0]
    total = pair_sum(partial_grad(jnp.swapaxes(gradient, 1, 2)[0], projection, weight), "c")
    half = total.shape[0] // 2
    total = lax.dynamic_slice_in_dim(total, lax.axis_index("c") * half, half, 0)
    for axis in ("l0", "l1", "l2"):
        total = pair_sum(total, axis)
    total = lax.all_gather(total, "c", axis=0, tiled=True)

    new_first, new_second, normalized, message = adam_and_norm(
        total, first_moment.T, second_moment.T, projection, lax.axis_size(PLANE)
    )
    position = lax.axis_index(REPLICA)
    own_projection = lax.dynamic_slice_in_dim(projection, position * rows_here, rows_here, 0)
    step = jnp.dot(
        own_projection, normalized.T, precision=lax.Precision.HIGHEST, preferred_element_type=jnp.float32
    )
    parts = jnp.sum(lax.all_to_all(message, PLANE, 0, 0), axis=0)
    return (scaled(blocks_sum(parts), step), new_first.T, new_second.T)


def solution(mesh):
    fine = Mesh(mesh.devices.reshape((2,) * 10), SHARD + REPLICA)
    placed = (
        P(REPLICA, None, SHARD),
        P(),
        P(None, SHARD),
        P(None, SHARD),
        P(REPLICA, SHARD),
    )
    return jax.shard_map(
        shards,
        mesh=fine,
        in_specs=placed,
        out_specs=(P(REPLICA, SHARD), P(None, SHARD), P(None, SHARD)),
        check_vma=False,
    )
```

```python
import functools

import jax
import jax.numpy as jnp
from jax import lax
from jax.experimental import pallas as pl
from jax.experimental.pallas import tpu as pltpu
from jax.sharding import Mesh, PartitionSpec as P

ADAM_STEP = 10
PLANE = ("y1", "y0", "x1", "x0")
BLOCKS = ("h1", "h0")
SHARD = BLOCKS + PLANE
REPLICA = ("l2", "l1", "l0", "c")
SUBLANES, LANES = 8, 128
MIB = 2**20


def partial_kernel(chunks, gradient, projection, weight, out, grad_v, proj_v, weight_v, sems):
    columns, depth = grad_v.shape
    depth //= chunks
    copies = []
    for i in range(chunks):
        part = pl.ds(i * depth, depth)
        copies.append(
            (
                pltpu.make_async_copy(projection.at[part], proj_v.at[part], sems.at[0, i]),
                pltpu.make_async_copy(gradient.at[:, part], grad_v.at[:, part], sems.at[1, i]),
            )
        )
        for copy in copies[-1]:
            copy.start()
    weight_copy = pltpu.make_async_copy(weight, weight_v, sems.at[2, 0])
    weight_copy.start()
    total = None
    for i in range(chunks):
        for copy in copies[i]:
            copy.wait()
        part = slice(i * depth, (i + 1) * depth)
        term = jnp.dot(
            grad_v[:, part], proj_v[part].astype(jnp.bfloat16), preferred_element_type=jnp.float32
        )
        total = term if total is None else total + term
    out[:columns] = total
    weight_copy.wait()
    weight_sq = jnp.sum(weight_v[...] * weight_v[...])
    out[columns:] = jnp.full((out.shape[0] - columns, out.shape[1]), weight_sq, jnp.float32)


def partial_grad(gradient, projection, weight):
    columns, depth = gradient.shape
    rank = projection.shape[1]
    chunks = 5
    anywhere = pl.BlockSpec(memory_space=pl.ANY)
    return pl.pallas_call(
        functools.partial(partial_kernel, chunks),
        out_shape=jax.ShapeDtypeStruct((columns + SUBLANES, rank), jnp.float32),
        in_specs=[anywhere] * 3,
        out_specs=pl.BlockSpec(memory_space=pltpu.VMEM),
        scratch_shapes=[
            pltpu.VMEM(gradient.shape, gradient.dtype),
            pltpu.VMEM(projection.shape, projection.dtype),
            pltpu.VMEM(weight.shape, weight.dtype),
            pltpu.SemaphoreType.DMA((3, chunks)),
        ],
        compiler_params=pltpu.CompilerParams(vmem_limit_bytes=60 * MIB),
    )(gradient, projection, weight)


def split(x):
    high = x.astype(jnp.bfloat16)
    low = (x - high.astype(jnp.float32)).astype(jnp.bfloat16)
    return high, low


def dot_rows(left, right):
    return lax.dot_general(
        left, right, (((1,), (1,)), ((), ())), preferred_element_type=jnp.float32
    )


def adam_kernel(total, first, second, projection, new_first, new_second, normal, message):
    columns = first.shape[0]
    low_grad = total[:columns]
    moment = 0.9 * first[...] + 0.1 * low_grad
    square = 0.95 * second[...] + 0.05 * low_grad * low_grad
    new_first[...] = moment
    new_second[...] = square
    first_fix = 1.0 - 0.9**ADAM_STEP
    second_fix = 1.0 - 0.95**ADAM_STEP
    normalized = moment / first_fix / (jnp.sqrt(square / second_fix) + 1e-08)
    normal[...] = normalized
    high, low = split(normalized)
    twice = jnp.concatenate([high, high], axis=1)
    depth = 512
    squares = jnp.zeros((SUBLANES, columns), jnp.float32)
    for i in range(projection.shape[0] // depth):
        left, left_low = split(projection[i * depth : (i + 1) * depth])
        step = dot_rows(jnp.concatenate([left, left_low], axis=1), twice) + dot_rows(left, low)
        squares += jnp.sum((step * step).reshape(depth // SUBLANES, SUBLANES, columns), axis=0)
    step_sq = jnp.sum(squares)
    lane = lax.broadcasted_iota(jnp.int32, (1, LANES), 1)
    row = jnp.where(lane == 0, step_sq, total[columns : columns + 1])
    message[...] = jnp.broadcast_to(row[None], message.shape)


def adam_and_norm(total, first, second, projection, partners):
    vmem = pl.BlockSpec(memory_space=pltpu.VMEM)
    shape = jax.ShapeDtypeStruct(first.shape, jnp.float32)
    return pl.pallas_call(
        adam_kernel,
        out_shape=(shape, shape, shape, jax.ShapeDtypeStruct((partners, 1, LANES), jnp.float32)),
        in_specs=[vmem] * 4,
        out_specs=(vmem,) * 4,
        compiler_params=pltpu.CompilerParams(vmem_limit_bytes=24 * MIB),
    )(total, first, second, projection)


def scale_kernel(sums, step, update):
    weight_sq = jnp.broadcast_to(sums[:, 1:2], (1, step.shape[1]))
    step_sq = jnp.broadcast_to(sums[:, :1], (1, step.shape[1]))
    update[...] = step[...] * (jnp.sqrt(weight_sq) / (jnp.sqrt(step_sq) + 1e-06))


def scaled(sums, step):
    vmem = pl.BlockSpec(memory_space=pltpu.VMEM)
    return pl.pallas_call(
        scale_kernel,
        out_shape=jax.ShapeDtypeStruct(step.shape, jnp.float32),
        in_specs=[vmem] * 2,
        out_specs=vmem,
        compiler_params=pltpu.CompilerParams(vmem_limit_bytes=16 * MIB),
    )(sums, step)


def pair_sum(x, axis):
    both = lax.all_gather(x, axis, axis=0, tiled=False)
    return both[0] + both[1]


def chip_permute(x, moves):
    cores = lax.axis_size("c")
    pairs = [(a * cores + c, b * cores + c) for a, b in moves for c in range(cores)]
    return lax.ppermute(x, BLOCKS + REPLICA, pairs)


def run(source, target, count):
    return [(source + i, target + i) for i in range(count)]


def blocks_sum(x):
    blocks, chips = lax.axis_size(BLOCKS), lax.axis_size(REPLICA[:3])
    half = chips // 2
    mirrored = [(2 * chips + i, chips - 1 - i) for i in range(chips)]
    total = x
    for moves in (run(chips, 0, chips), mirrored, run(3 * chips, 0, chips)):
        total = total + chip_permute(x, moves)
    place = lax.axis_index(BLOCKS + REPLICA[:3])
    steps = (
        run(half, chips, half),
        run(chips, 2 * chips, half) + run(half, blocks * chips - half, half),
        run(chips, chips + half, half)
        + run(2 * chips, 2 * chips + half, half)
        + run(blocks * chips - half, 3 * chips, half),
    )
    for moves in steps:
        starts = {target for _, target in moves if target % half == 0}
        arrived = chip_permute(total, moves)
        new = functools.reduce(
            jnp.logical_or, [(place >= start) & (place < start + half) for start in sorted(starts)]
        )
        total = jnp.where(new, arrived, total)
    return total


def shards(gradient, projection, first_moment, second_moment, weight):
    rows_here = weight.shape[0]
    total = pair_sum(partial_grad(jnp.swapaxes(gradient, 1, 2)[0], projection, weight), "c")
    half = total.shape[0] // 2
    total = lax.dynamic_slice_in_dim(total, lax.axis_index("c") * half, half, 0)
    for axis in ("l0", "l1", "l2"):
        total = pair_sum(total, axis)
    total = lax.all_gather(total, "c", axis=0, tiled=True)

    new_first, new_second, normalized, message = adam_and_norm(
        total, first_moment.T, second_moment.T, projection, lax.axis_size(PLANE)
    )
    position = lax.axis_index(REPLICA)
    own_projection = lax.dynamic_slice_in_dim(projection, position * rows_here, rows_here, 0)
    step = jnp.dot(
        own_projection, normalized.T, precision=lax.Precision.HIGHEST, preferred_element_type=jnp.float32
    )
    parts = jnp.sum(lax.all_to_all(message, PLANE, 0, 0), axis=0)
    return (scaled(blocks_sum(parts), step), new_first.T, new_second.T)


def solution(mesh):
    fine = Mesh(mesh.devices.reshape((2,) * 10), SHARD + REPLICA)
    placed = (
        P(REPLICA, None, SHARD),
        P(),
        P(None, SHARD),
        P(None, SHARD),
        P(REPLICA, SHARD),
    )
    return jax.shard_map(
        shards,
        mesh=fine,
        in_specs=placed,
        out_specs=(P(REPLICA, SHARD), P(None, SHARD), P(None, SHARD)),
        check_vma=False,
    )
```

```python
import functools

import jax
import jax.numpy as jnp
from jax import lax
from jax.experimental import pallas as pl
from jax.experimental.pallas import tpu as pltpu
from jax.sharding import Mesh, PartitionSpec as P

ADAM_STEP = 10
PLANE = ("y1", "y0", "x1", "x0")
BLOCKS = ("h1", "h0")
SHARD = BLOCKS + PLANE
REPLICA = ("l2", "l1", "l0", "c")
SUBLANES, LANES = 8, 128
MIB = 2**20


def partial_kernel(chunks, gradient, projection, weight, out, grad_v, proj_v, weight_v, sems):
    columns, depth = grad_v.shape
    depth //= chunks
    copies = []
    for i in range(chunks):
        part = pl.ds(i * depth, depth)
        copies.append(
            (
                pltpu.make_async_copy(projection.at[part], proj_v.at[part], sems.at[0, i]),
                pltpu.make_async_copy(gradient.at[:, part], grad_v.at[:, part], sems.at[1, i]),
            )
        )
        for copy in copies[-1]:
            copy.start()
    weight_copy = pltpu.make_async_copy(weight, weight_v, sems.at[2, 0])
    weight_copy.start()
    total = None
    for i in range(chunks):
        for copy in copies[i]:
            copy.wait()
        part = slice(i * depth, (i + 1) * depth)
        term = jnp.dot(
            grad_v[:, part], proj_v[part].astype(jnp.bfloat16), preferred_element_type=jnp.float32
        )
        total = term if total is None else total + term
    out[:columns] = total
    weight_copy.wait()
    weight_sq = jnp.sum(weight_v[...] * weight_v[...])
    out[columns:] = jnp.full((out.shape[0] - columns, out.shape[1]), weight_sq, jnp.float32)


def partial_grad(gradient, projection, weight):
    columns, depth = gradient.shape
    rank = projection.shape[1]
    chunks = 5
    anywhere = pl.BlockSpec(memory_space=pl.ANY)
    return pl.pallas_call(
        functools.partial(partial_kernel, chunks),
        out_shape=jax.ShapeDtypeStruct((columns + SUBLANES, rank), jnp.float32),
        in_specs=[anywhere] * 3,
        out_specs=pl.BlockSpec(memory_space=pltpu.VMEM),
        scratch_shapes=[
            pltpu.VMEM(gradient.shape, gradient.dtype),
            pltpu.VMEM(projection.shape, projection.dtype),
            pltpu.VMEM(weight.shape, weight.dtype),
            pltpu.SemaphoreType.DMA((3, chunks)),
        ],
        compiler_params=pltpu.CompilerParams(vmem_limit_bytes=60 * MIB),
    )(gradient, projection, weight)


def split(x):
    high = x.astype(jnp.bfloat16)
    low = (x - high.astype(jnp.float32)).astype(jnp.bfloat16)
    return high, low


def dot_rows(left, right):
    return lax.dot_general(
        left, right, (((1,), (1,)), ((), ())), preferred_element_type=jnp.float32
    )


def adam_kernel(total, first, second, projection, new_first, new_second, normal, message):
    columns = first.shape[0]
    low_grad = total[:columns]
    moment = 0.9 * first[...] + 0.1 * low_grad
    square = 0.95 * second[...] + 0.05 * low_grad * low_grad
    new_first[...] = moment
    new_second[...] = square
    first_fix = 1.0 - 0.9**ADAM_STEP
    second_fix = 1.0 - 0.95**ADAM_STEP
    normalized = moment / first_fix / (jnp.sqrt(square / second_fix) + 1e-08)
    normal[...] = normalized
    high, low = split(normalized)
    right = jnp.concatenate([high, high, low], axis=1)
    depth = 512
    squares = jnp.zeros((SUBLANES, columns), jnp.float32)
    for i in range(projection.shape[0] // depth):
        left, left_low = split(projection[i * depth : (i + 1) * depth])
        step = dot_rows(jnp.concatenate([left, left_low, left], axis=1), right)
        squares += jnp.sum((step * step).reshape(depth // SUBLANES, SUBLANES, columns), axis=0)
    step_sq = jnp.sum(squares)
    lane = lax.broadcasted_iota(jnp.int32, (1, LANES), 1)
    row = jnp.where(lane == 0, step_sq, total[columns : columns + 1])
    message[...] = jnp.broadcast_to(row[None], message.shape)


def adam_and_norm(total, first, second, projection, partners):
    vmem = pl.BlockSpec(memory_space=pltpu.VMEM)
    shape = jax.ShapeDtypeStruct(first.shape, jnp.float32)
    return pl.pallas_call(
        adam_kernel,
        out_shape=(shape, shape, shape, jax.ShapeDtypeStruct((partners, 1, LANES), jnp.float32)),
        in_specs=[vmem] * 4,
        out_specs=(vmem,) * 4,
        compiler_params=pltpu.CompilerParams(vmem_limit_bytes=24 * MIB),
    )(total, first, second, projection)


def scale_kernel(sums, step, update):
    weight_sq = jnp.broadcast_to(sums[:, 1:2], (1, step.shape[1]))
    step_sq = jnp.broadcast_to(sums[:, :1], (1, step.shape[1]))
    update[...] = step[...] * (jnp.sqrt(weight_sq) / (jnp.sqrt(step_sq) + 1e-06))


def scaled(sums, step):
    vmem = pl.BlockSpec(memory_space=pltpu.VMEM)
    return pl.pallas_call(
        scale_kernel,
        out_shape=jax.ShapeDtypeStruct(step.shape, jnp.float32),
        in_specs=[vmem] * 2,
        out_specs=vmem,
        compiler_params=pltpu.CompilerParams(vmem_limit_bytes=16 * MIB),
    )(sums, step)


def pair_sum(x, axis):
    both = lax.all_gather(x, axis, axis=0, tiled=False)
    return both[0] + both[1]


def chip_permute(x, moves):
    cores = lax.axis_size("c")
    pairs = [(a * cores + c, b * cores + c) for a, b in moves for c in range(cores)]
    return lax.ppermute(x, BLOCKS + REPLICA, pairs)


def run(source, target, count):
    return [(source + i, target + i) for i in range(count)]


def blocks_sum(x):
    blocks, chips = lax.axis_size(BLOCKS), lax.axis_size(REPLICA[:3])
    half = chips // 2
    mirrored = [(2 * chips + i, chips - 1 - i) for i in range(chips)]
    total = x
    for moves in (run(chips, 0, chips), mirrored, run(3 * chips, 0, chips)):
        total = total + chip_permute(x, moves)
    place = lax.axis_index(BLOCKS + REPLICA[:3])
    steps = (
        run(half, chips, half),
        run(chips, 2 * chips, half) + run(half, blocks * chips - half, half),
        run(chips, chips + half, half)
        + [(half + i, 3 * chips - 1 - i) for i in range(half)]
        + run(blocks * chips - half, 3 * chips, half),
    )
    for moves in steps:
        starts = {target for _, target in moves if target % half == 0}
        arrived = chip_permute(total, moves)
        new = functools.reduce(
            jnp.logical_or, [(place >= start) & (place < start + half) for start in sorted(starts)]
        )
        total = jnp.where(new, arrived, total)
    return total


def shards(gradient, projection, first_moment, second_moment, weight):
    rows_here = weight.shape[0]
    total = pair_sum(partial_grad(jnp.swapaxes(gradient, 1, 2)[0], projection, weight), "c")
    half = total.shape[0] // 2
    total = lax.dynamic_slice_in_dim(total, lax.axis_index("c") * half, half, 0)
    for axis in ("l0", "l1", "l2"):
        total = pair_sum(total, axis)
    total = lax.all_gather(total, "c", axis=0, tiled=True)

    new_first, new_second, normalized, message = adam_and_norm(
        total, first_moment.T, second_moment.T, projection, lax.axis_size(PLANE)
    )
    position = lax.axis_index(REPLICA)
    own_projection = lax.dynamic_slice_in_dim(projection, position * rows_here, rows_here, 0)
    step = jnp.dot(
        own_projection, normalized.T, precision=lax.Precision.HIGHEST, preferred_element_type=jnp.float32
    )
    parts = jnp.sum(lax.all_to_all(message, PLANE, 0, 0), axis=0)
    return (scaled(blocks_sum(parts), step), new_first.T, new_second.T)


def solution(mesh):
    fine = Mesh(mesh.devices.reshape((2,) * 10), SHARD + REPLICA)
    placed = (
        P(REPLICA, None, SHARD),
        P(),
        P(None, SHARD),
        P(None, SHARD),
        P(REPLICA, SHARD),
    )
    return jax.shard_map(
        shards,
        mesh=fine,
        in_specs=placed,
        out_specs=(P(REPLICA, SHARD), P(None, SHARD), P(None, SHARD)),
        check_vma=False,
    )
```

```python
import functools

import jax
import jax.numpy as jnp
from jax import lax
from jax.experimental import pallas as pl
from jax.experimental.pallas import tpu as pltpu
from jax.sharding import Mesh, PartitionSpec as P

ADAM_STEP = 10
PLANE = ("y1", "y0", "x1", "x0")
BLOCKS = ("h1", "h0")
SHARD = BLOCKS + PLANE
REPLICA = ("l2", "l1", "l0", "c")
SUBLANES, LANES = 8, 128
MIB = 2**20


def partial_kernel(chunks, gradient, projection, weight, out, grad_v, proj_v, weight_v, sems):
    columns, depth = grad_v.shape
    depth //= chunks
    copies = []
    for i in range(chunks):
        part = pl.ds(i * depth, depth)
        copies.append(
            (
                pltpu.make_async_copy(projection.at[part], proj_v.at[part], sems.at[0, i]),
                pltpu.make_async_copy(gradient.at[:, part], grad_v.at[:, part], sems.at[1, i]),
            )
        )
        for copy in copies[-1]:
            copy.start()
    weight_copy = pltpu.make_async_copy(weight, weight_v, sems.at[2, 0])
    weight_copy.start()
    total = None
    for i in range(chunks):
        for copy in copies[i]:
            copy.wait()
        part = slice(i * depth, (i + 1) * depth)
        term = jnp.dot(
            grad_v[:, part], proj_v[part].astype(jnp.bfloat16), preferred_element_type=jnp.float32
        )
        total = term if total is None else total + term
    out[:columns] = total
    weight_copy.wait()
    weight_sq = jnp.sum(weight_v[...] * weight_v[...])
    out[columns:] = jnp.full((out.shape[0] - columns, out.shape[1]), weight_sq, jnp.float32)


def partial_grad(gradient, projection, weight):
    columns, depth = gradient.shape
    rank = projection.shape[1]
    chunks = 5
    anywhere = pl.BlockSpec(memory_space=pl.ANY)
    return pl.pallas_call(
        functools.partial(partial_kernel, chunks),
        out_shape=jax.ShapeDtypeStruct((columns + SUBLANES, rank), jnp.float32),
        in_specs=[anywhere] * 3,
        out_specs=pl.BlockSpec(memory_space=pltpu.VMEM),
        scratch_shapes=[
            pltpu.VMEM(gradient.shape, gradient.dtype),
            pltpu.VMEM(projection.shape, projection.dtype),
            pltpu.VMEM(weight.shape, weight.dtype),
            pltpu.SemaphoreType.DMA((3, chunks)),
        ],
        compiler_params=pltpu.CompilerParams(vmem_limit_bytes=60 * MIB),
    )(gradient, projection, weight)


def split(x):
    high = x.astype(jnp.bfloat16)
    low = (x - high.astype(jnp.float32)).astype(jnp.bfloat16)
    return high, low


def dot_rows(left, right):
    return lax.dot_general(
        left, right, (((1,), (1,)), ((), ())), preferred_element_type=jnp.float32
    )


def adam_kernel(total, first, second, projection, new_first, new_second, normal, message):
    columns = first.shape[0]
    low_grad = total[:columns]
    moment = 0.9 * first[...] + 0.1 * low_grad
    square = 0.95 * second[...] + 0.05 * low_grad * low_grad
    new_first[...] = moment
    new_second[...] = square
    first_fix = 1.0 - 0.9**ADAM_STEP
    second_fix = 1.0 - 0.95**ADAM_STEP
    normalized = moment / first_fix / (jnp.sqrt(square / second_fix) + 1e-08)
    normal[...] = normalized
    high, low = split(normalized)
    right = jnp.concatenate([high, high, low], axis=1)
    depth = 512
    squares = jnp.zeros((SUBLANES, columns), jnp.float32)
    for i in range(projection.shape[0] // depth):
        left, left_low = split(projection[i * depth : (i + 1) * depth])
        step = dot_rows(jnp.concatenate([left, left_low, left], axis=1), right)
        squares += jnp.sum((step * step).reshape(depth // SUBLANES, SUBLANES, columns), axis=0)
    step_sq = jnp.sum(squares)
    lane = lax.broadcasted_iota(jnp.int32, (1, LANES), 1)
    row = jnp.where(lane == 0, step_sq, total[columns : columns + 1])
    message[...] = jnp.broadcast_to(row[None], message.shape)


def adam_and_norm(total, first, second, projection, partners):
    vmem = pl.BlockSpec(memory_space=pltpu.VMEM)
    shape = jax.ShapeDtypeStruct(first.shape, jnp.float32)
    return pl.pallas_call(
        adam_kernel,
        out_shape=(shape, shape, shape, jax.ShapeDtypeStruct((partners, 1, LANES), jnp.float32)),
        in_specs=[vmem] * 4,
        out_specs=(vmem,) * 4,
        compiler_params=pltpu.CompilerParams(vmem_limit_bytes=24 * MIB),
    )(total, first, second, projection)


def scale_kernel(sums, step, update):
    weight_sq = jnp.broadcast_to(sums[:, 1:2], (1, step.shape[1]))
    step_sq = jnp.broadcast_to(sums[:, :1], (1, step.shape[1]))
    update[...] = step[...] * (jnp.sqrt(weight_sq) / (jnp.sqrt(step_sq) + 1e-06))


def scaled(sums, step):
    vmem = pl.BlockSpec(memory_space=pltpu.VMEM)
    return pl.pallas_call(
        scale_kernel,
        out_shape=jax.ShapeDtypeStruct(step.shape, jnp.float32),
        in_specs=[vmem] * 2,
        out_specs=vmem,
        compiler_params=pltpu.CompilerParams(vmem_limit_bytes=16 * MIB),
    )(sums, step)


def pair_sum(x, axis):
    both = lax.all_gather(x, axis, axis=0, tiled=False)
    return both[0] + both[1]


SPREAD = (
    ((7, 8), (6, 9), (5, 10), (4, 11)),
    ((8, 16), (9, 17), (10, 18), (11, 19), (7, 29), (6, 30), (5, 31), (4, 28)),
    ((8, 12), (9, 13), (10, 14), (11, 15), (16, 20), (17, 21), (7, 22), (6, 23), (31, 24), (28, 25), (30, 26), (29, 27)),
)


def chip_permute(x, moves):
    cores = lax.axis_size("c")
    pairs = [(a * cores + c, b * cores + c) for a, b in moves for c in range(cores)]
    return lax.ppermute(x, BLOCKS + REPLICA, pairs)


def run(source, target, count):
    return [(source + i, target + i) for i in range(count)]


def blocks_sum(x):
    chips = lax.axis_size(REPLICA[:3])
    half = chips // 2
    mirrored = [(2 * chips + i, chips - 1 - i) for i in range(chips)]
    total = x
    for moves in (run(chips, 0, chips), mirrored, run(3 * chips, 0, chips)):
        total = total + chip_permute(x, moves)
    place = lax.axis_index(BLOCKS + REPLICA[:3])
    for moves in SPREAD:
        targets = {target - target % half for _, target in moves}
        arrived = chip_permute(total, moves)
        new = functools.reduce(
            jnp.logical_or, [(place >= start) & (place < start + half) for start in sorted(targets)]
        )
        total = jnp.where(new, arrived, total)
    return total


def shards(gradient, projection, first_moment, second_moment, weight):
    rows_here = weight.shape[0]
    total = pair_sum(partial_grad(jnp.swapaxes(gradient, 1, 2)[0], projection, weight), "c")
    half = total.shape[0] // 2
    total = lax.dynamic_slice_in_dim(total, lax.axis_index("c") * half, half, 0)
    for axis in ("l0", "l1", "l2"):
        total = pair_sum(total, axis)
    total = lax.all_gather(total, "c", axis=0, tiled=True)

    new_first, new_second, normalized, message = adam_and_norm(
        total, first_moment.T, second_moment.T, projection, lax.axis_size(PLANE)
    )
    position = lax.axis_index(REPLICA)
    own_projection = lax.dynamic_slice_in_dim(projection, position * rows_here, rows_here, 0)
    step = jnp.dot(
        own_projection, normalized.T, precision=lax.Precision.HIGHEST, preferred_element_type=jnp.float32
    )
    parts = jnp.sum(lax.all_to_all(message, PLANE, 0, 0), axis=0)
    return (scaled(blocks_sum(parts), step), new_first.T, new_second.T)


def solution(mesh):
    fine = Mesh(mesh.devices.reshape((2,) * 10), SHARD + REPLICA)
    placed = (
        P(REPLICA, None, SHARD),
        P(),
        P(None, SHARD),
        P(None, SHARD),
        P(REPLICA, SHARD),
    )
    return jax.shard_map(
        shards,
        mesh=fine,
        in_specs=placed,
        out_specs=(P(REPLICA, SHARD), P(None, SHARD), P(None, SHARD)),
        check_vma=False,
    )
```

```python
import functools

import jax
import jax.numpy as jnp
from jax import lax
from jax.experimental import pallas as pl
from jax.experimental.pallas import tpu as pltpu
from jax.sharding import Mesh, PartitionSpec as P

ADAM_STEP = 10
PLANE = ("y1", "y0", "x1", "x0")
BLOCKS = ("h1", "h0")
SHARD = BLOCKS + PLANE
REPLICA = ("l2", "l1", "l0", "c")
SUBLANES, LANES = 8, 128
MIB = 2**20


def partial_kernel(chunks, gradient, projection, weight, out, grad_v, proj_v, weight_v, sems):
    columns, depth = grad_v.shape
    depth //= chunks
    copies = []
    weight_copy = pltpu.make_async_copy(weight, weight_v, sems.at[2, 0])
    for i in range(chunks):
        part = pl.ds(i * depth, depth)
        copies.append(
            (
                pltpu.make_async_copy(projection.at[part], proj_v.at[part], sems.at[0, i]),
                pltpu.make_async_copy(gradient.at[:, part], grad_v.at[:, part], sems.at[1, i]),
            )
        )
        for copy in copies[-1]:
            copy.start()
        if i == 1:
            weight_copy.start()
    total = None
    for i in range(chunks):
        if i == chunks - 1:
            weight_copy.wait()
            weight_sq = jnp.sum(weight_v[...] * weight_v[...], axis=(0, 1), keepdims=True)
        for copy in copies[i]:
            copy.wait()
        part = slice(i * depth, (i + 1) * depth)
        term = jnp.dot(
            grad_v[:, part], proj_v[part].astype(jnp.bfloat16), preferred_element_type=jnp.float32
        )
        total = term if total is None else total + term
    out[:columns] = total
    out[columns:] = jnp.broadcast_to(weight_sq, (out.shape[0] - columns, out.shape[1]))


def partial_grad(gradient, projection, weight):
    columns, depth = gradient.shape
    rank = projection.shape[1]
    chunks = 5
    anywhere = pl.BlockSpec(memory_space=pl.ANY)
    return pl.pallas_call(
        functools.partial(partial_kernel, chunks),
        out_shape=jax.ShapeDtypeStruct((columns + SUBLANES, rank), jnp.float32),
        in_specs=[anywhere] * 3,
        out_specs=pl.BlockSpec(memory_space=pltpu.VMEM),
        scratch_shapes=[
            pltpu.VMEM(gradient.shape, gradient.dtype),
            pltpu.VMEM(projection.shape, projection.dtype),
            pltpu.VMEM(weight.shape, weight.dtype),
            pltpu.SemaphoreType.DMA((3, chunks)),
        ],
        compiler_params=pltpu.CompilerParams(vmem_limit_bytes=60 * MIB),
    )(gradient, projection, weight)


def split(x):
    high = x.astype(jnp.bfloat16)
    low = (x - high.astype(jnp.float32)).astype(jnp.bfloat16)
    return high, low


def dot_rows(left, right):
    return lax.dot_general(
        left, right, (((1,), (1,)), ((), ())), preferred_element_type=jnp.float32
    )


def new_moments(low_grad, first, second):
    return 0.9 * first + 0.1 * low_grad, 0.95 * second + 0.05 * low_grad * low_grad


def norm_kernel(total, first, second, projection, normal, message):
    columns = first.shape[0]
    moment, square = new_moments(total[:columns], first[...], second[...])
    first_fix = 1.0 - 0.9**ADAM_STEP
    second_fix = 1.0 - 0.95**ADAM_STEP
    normalized = moment / first_fix / (jnp.sqrt(square / second_fix) + 1e-08)
    normal[...] = normalized
    high, low = split(normalized)
    right = jnp.concatenate([high, high, low], axis=1)
    depth = 512
    squares = jnp.zeros((SUBLANES, columns), jnp.float32)
    for i in range(projection.shape[0] // depth):
        left, left_low = split(projection[i * depth : (i + 1) * depth])
        step = dot_rows(jnp.concatenate([left, left_low, left], axis=1), right)
        squares += jnp.sum((step * step).reshape(depth // SUBLANES, SUBLANES, columns), axis=0)
    step_sq = jnp.sum(squares, axis=(0, 1), keepdims=True)
    lane = lax.broadcasted_iota(jnp.int32, (1, LANES), 1)
    row = jnp.where(lane == 0, step_sq, total[columns : columns + 1])
    message[...] = jnp.broadcast_to(row[None], message.shape)


def normal_and_norm(total, first, second, projection, partners):
    vmem = pl.BlockSpec(memory_space=pltpu.VMEM)
    shape = jax.ShapeDtypeStruct(first.shape, jnp.float32)
    return pl.pallas_call(
        norm_kernel,
        out_shape=(shape, jax.ShapeDtypeStruct((partners, 1, LANES), jnp.float32)),
        in_specs=[vmem] * 4,
        out_specs=(vmem,) * 2,
        compiler_params=pltpu.CompilerParams(vmem_limit_bytes=24 * MIB),
    )(total, first, second, projection)


def scale_kernel(sums, step, update):
    weight_sq = jnp.broadcast_to(sums[:, 1:2], (1, step.shape[1]))
    step_sq = jnp.broadcast_to(sums[:, :1], (1, step.shape[1]))
    update[...] = step[...] * (jnp.sqrt(weight_sq) / (jnp.sqrt(step_sq) + 1e-06))


def scaled(sums, step):
    vmem = pl.BlockSpec(memory_space=pltpu.VMEM)
    return pl.pallas_call(
        scale_kernel,
        out_shape=jax.ShapeDtypeStruct(step.shape, jnp.float32),
        in_specs=[vmem] * 2,
        out_specs=vmem,
        compiler_params=pltpu.CompilerParams(vmem_limit_bytes=16 * MIB),
    )(sums, step)


def pair_sum(x, axis):
    both = lax.all_gather(x, axis, axis=0, tiled=False)
    return both[0] + both[1]


SPREAD = (
    ((7, 8), (6, 9), (5, 10), (4, 11)),
    ((8, 16), (9, 17), (10, 18), (11, 19), (7, 29), (6, 30), (5, 31), (4, 28)),
    ((8, 12), (9, 13), (10, 14), (11, 15), (16, 20), (17, 21), (7, 22), (6, 23), (31, 24), (28, 25), (30, 26), (29, 27)),
)


def chip_permute(x, moves):
    cores = lax.axis_size("c")
    pairs = [(a * cores + c, b * cores + c) for a, b in moves for c in range(cores)]
    return lax.ppermute(x, BLOCKS + REPLICA, pairs)


def run(source, target, count):
    return [(source + i, target + i) for i in range(count)]


def blocks_sum(x):
    chips = lax.axis_size(REPLICA[:3])
    half = chips // 2
    mirrored = [(2 * chips + i, chips - 1 - i) for i in range(chips)]
    total = x
    for moves in (run(chips, 0, chips), mirrored, run(3 * chips, 0, chips)):
        total = total + chip_permute(x, moves)
    place = lax.axis_index(BLOCKS + REPLICA[:3])
    for moves in SPREAD:
        targets = {target - target % half for _, target in moves}
        arrived = chip_permute(total, moves)
        new = functools.reduce(
            jnp.logical_or, [(place >= start) & (place < start + half) for start in sorted(targets)]
        )
        total = jnp.where(new, arrived, total)
    return total


def shards(gradient, projection, first_moment, second_moment, weight):
    rows_here = weight.shape[0]
    total = pair_sum(partial_grad(jnp.swapaxes(gradient, 1, 2)[0], projection, weight), "c")
    half = total.shape[0] // 2
    total = lax.dynamic_slice_in_dim(total, lax.axis_index("c") * half, half, 0)
    for axis in ("l0", "l1", "l2"):
        total = pair_sum(total, axis)
    total = lax.all_gather(total, "c", axis=0, tiled=True)

    first, second = first_moment.T, second_moment.T
    normalized, message = normal_and_norm(total, first, second, projection, lax.axis_size(PLANE))
    new_first, new_second = new_moments(total[: first.shape[0]], first, second)
    position = lax.axis_index(REPLICA)
    own_projection = lax.dynamic_slice_in_dim(projection, position * rows_here, rows_here, 0)
    step = jnp.dot(
        own_projection, normalized.T, precision=lax.Precision.HIGHEST, preferred_element_type=jnp.float32
    )
    parts = jnp.sum(lax.all_to_all(message, PLANE, 0, 0), axis=0)
    return (scaled(blocks_sum(parts), step), new_first.T, new_second.T)


def solution(mesh):
    fine = Mesh(mesh.devices.reshape((2,) * 10), SHARD + REPLICA)
    placed = (
        P(REPLICA, None, SHARD),
        P(),
        P(None, SHARD),
        P(None, SHARD),
        P(REPLICA, SHARD),
    )
    return jax.shard_map(
        shards,
        mesh=fine,
        in_specs=placed,
        out_specs=(P(REPLICA, SHARD), P(None, SHARD), P(None, SHARD)),
        check_vma=False,
    )
```

```python
import functools

import jax
import jax.numpy as jnp
from jax import lax
from jax.experimental import pallas as pl
from jax.experimental.pallas import tpu as pltpu
from jax.sharding import Mesh, PartitionSpec as P

ADAM_STEP = 10
PLANE = ("y1", "y0", "x1", "x0")
BLOCKS = ("h1", "h0")
SHARD = BLOCKS + PLANE
REPLICA = ("l2", "l1", "l0", "c")
SUBLANES, LANES = 8, 128
MIB = 2**20


def partial_kernel(chunks, gradient, projection, weight, out, grad_v, proj_v, weight_v, sems):
    columns, depth = grad_v.shape
    depth //= chunks
    copies = []
    weight_copy = pltpu.make_async_copy(weight, weight_v, sems.at[2, 0])
    for i in range(chunks):
        part = pl.ds(i * depth, depth)
        copies.append(
            (
                pltpu.make_async_copy(projection.at[part], proj_v.at[part], sems.at[0, i]),
                pltpu.make_async_copy(gradient.at[:, part], grad_v.at[:, part], sems.at[1, i]),
            )
        )
        for copy in copies[-1]:
            copy.start()
        if i == 1:
            weight_copy.start()
    total = None
    for i in range(chunks):
        if i == chunks - 1:
            weight_copy.wait()
            weight_sq = jnp.sum(weight_v[...] * weight_v[...], axis=(0, 1), keepdims=True)
        for copy in copies[i]:
            copy.wait()
        part = slice(i * depth, (i + 1) * depth)
        term = jnp.dot(
            grad_v[:, part], proj_v[part].astype(jnp.bfloat16), preferred_element_type=jnp.float32
        )
        total = term if total is None else total + term
    out[:columns] = total
    out[columns:] = jnp.broadcast_to(weight_sq, (out.shape[0] - columns, out.shape[1]))


def partial_grad(gradient, projection, weight):
    columns, depth = gradient.shape
    rank = projection.shape[1]
    chunks = 5
    anywhere = pl.BlockSpec(memory_space=pl.ANY)
    return pl.pallas_call(
        functools.partial(partial_kernel, chunks),
        out_shape=jax.ShapeDtypeStruct((columns + SUBLANES, rank), jnp.float32),
        in_specs=[anywhere] * 3,
        out_specs=pl.BlockSpec(memory_space=pltpu.VMEM),
        scratch_shapes=[
            pltpu.VMEM(gradient.shape, gradient.dtype),
            pltpu.VMEM(projection.shape, projection.dtype),
            pltpu.VMEM(weight.shape, weight.dtype),
            pltpu.SemaphoreType.DMA((3, chunks)),
        ],
        compiler_params=pltpu.CompilerParams(vmem_limit_bytes=60 * MIB),
    )(gradient, projection, weight)


def split(x):
    high = x.astype(jnp.bfloat16)
    low = (x - high.astype(jnp.float32)).astype(jnp.bfloat16)
    return high, low


def dot_rows(left, right):
    return lax.dot_general(
        left, right, (((1,), (1,)), ((), ())), preferred_element_type=jnp.float32
    )


def new_moments(low_grad, first, second):
    return 0.9 * first + 0.1 * low_grad, 0.95 * second + 0.05 * low_grad * low_grad


def norm_kernel(total, first, second, projection, normal, message):
    columns = first.shape[0]
    moment, square = new_moments(total[:columns], first[...], second[...])
    first_fix = 1.0 - 0.9**ADAM_STEP
    second_fix = 1.0 - 0.95**ADAM_STEP
    normalized = moment / first_fix / (jnp.sqrt(square / second_fix) + 1e-08)
    normal[...] = normalized
    high, low = split(normalized)
    right = jnp.concatenate([high, high, low], axis=1)
    depth = 512
    squares = jnp.zeros((SUBLANES, columns), jnp.float32)
    for i in range(projection.shape[0] // depth):
        left, left_low = split(projection[i * depth : (i + 1) * depth])
        step = dot_rows(jnp.concatenate([left, left_low, left], axis=1), right)
        squares += jnp.sum((step * step).reshape(depth // SUBLANES, SUBLANES, columns), axis=0)
    step_sq = jnp.sum(squares, axis=(0, 1), keepdims=True)
    lane = lax.broadcasted_iota(jnp.int32, (1, LANES), 1)
    row = jnp.where(lane == 0, step_sq, total[columns : columns + 1])
    message[...] = jnp.broadcast_to(row[None], message.shape)


def normal_and_norm(total, first, second, projection, partners):
    vmem = pl.BlockSpec(memory_space=pltpu.VMEM)
    shape = jax.ShapeDtypeStruct(first.shape, jnp.float32)
    return pl.pallas_call(
        norm_kernel,
        out_shape=(shape, jax.ShapeDtypeStruct((partners, 1, LANES), jnp.float32)),
        in_specs=[vmem] * 4,
        out_specs=(vmem,) * 2,
        compiler_params=pltpu.CompilerParams(vmem_limit_bytes=24 * MIB),
    )(total, first, second, projection)


def scale_kernel(sums, step, update):
    weight_sq = jnp.broadcast_to(sums[:, 1:2], (1, step.shape[1]))
    step_sq = jnp.broadcast_to(sums[:, :1], (1, step.shape[1]))
    update[...] = step[...] * (jnp.sqrt(weight_sq) / (jnp.sqrt(step_sq) + 1e-06))


def scaled(sums, step):
    vmem = pl.BlockSpec(memory_space=pltpu.VMEM)
    return pl.pallas_call(
        scale_kernel,
        out_shape=jax.ShapeDtypeStruct(step.shape, jnp.float32),
        in_specs=[vmem] * 2,
        out_specs=vmem,
        compiler_params=pltpu.CompilerParams(vmem_limit_bytes=16 * MIB),
    )(sums, step)


def pair_sum(x, axis):
    both = lax.all_gather(x, axis, axis=0, tiled=False)
    return both[0] + both[1]


SPREAD = (
    ((7, 8), (6, 9), (5, 10), (4, 11)),
    ((8, 16), (9, 17), (10, 18), (11, 19), (7, 29), (6, 30), (5, 31), (4, 28)),
    ((8, 12), (9, 13), (10, 14), (11, 15), (16, 20), (17, 21), (7, 22), (6, 23), (31, 24), (28, 25), (30, 26), (29, 27)),
)


def chip_permute(x, moves):
    cores = lax.axis_size("c")
    pairs = [(a * cores + c, b * cores + c) for a, b in moves for c in range(cores)]
    return lax.ppermute(x, BLOCKS + REPLICA, pairs)


def run(source, target, count):
    return [(source + i, target + i) for i in range(count)]


def blocks_sum(x):
    chips = lax.axis_size(REPLICA[:3])
    half = chips // 2
    mirrored = [(2 * chips + i, chips - 1 - i) for i in range(chips)]
    total = x
    for moves in (mirrored, run(3 * chips, 0, chips), run(chips, 0, chips)):
        total = total + chip_permute(x, moves)
    place = lax.axis_index(BLOCKS + REPLICA[:3])
    for moves in SPREAD:
        targets = {target - target % half for _, target in moves}
        arrived = chip_permute(total, moves)
        new = functools.reduce(
            jnp.logical_or, [(place >= start) & (place < start + half) for start in sorted(targets)]
        )
        total = jnp.where(new, arrived, total)
    return total


def shards(gradient, projection, first_moment, second_moment, weight):
    rows_here = weight.shape[0]
    total = pair_sum(partial_grad(jnp.swapaxes(gradient, 1, 2)[0], projection, weight), "c")
    half = total.shape[0] // 2
    total = lax.dynamic_slice_in_dim(total, lax.axis_index("c") * half, half, 0)
    for axis in ("l0", "l1", "l2"):
        total = pair_sum(total, axis)
    total = lax.all_gather(total, "c", axis=0, tiled=True)

    first, second = first_moment.T, second_moment.T
    normalized, message = normal_and_norm(total, first, second, projection, lax.axis_size(PLANE))
    new_first, new_second = new_moments(total[: first.shape[0]], first, second)
    position = lax.axis_index(REPLICA)
    own_projection = lax.dynamic_slice_in_dim(projection, position * rows_here, rows_here, 0)
    step = jnp.dot(
        own_projection, normalized.T, precision=lax.Precision.HIGHEST, preferred_element_type=jnp.float32
    )
    parts = jnp.sum(lax.all_to_all(message, PLANE, 0, 0), axis=0)
    return (scaled(blocks_sum(parts), step), new_first.T, new_second.T)


def solution(mesh):
    fine = Mesh(mesh.devices.reshape((2,) * 10), SHARD + REPLICA)
    placed = (
        P(REPLICA, None, SHARD),
        P(),
        P(None, SHARD),
        P(None, SHARD),
        P(REPLICA, SHARD),
    )
    return jax.shard_map(
        shards,
        mesh=fine,
        in_specs=placed,
        out_specs=(P(REPLICA, SHARD), P(None, SHARD), P(None, SHARD)),
        check_vma=False,
    )
```
